128 devices in a mesh: dp: 8 (over z, x_lo), seq: 16 (over y, x_hi, core).
Axes of the slice: x: 4 (x_hi: 2, x_lo: 2; x = x_hi * 2 + x_lo), y: 4, z: 4, core: 2. Of those that a mesh axis runs over, the one named last changes fastest.
Arguments:
- frames: bfloat16 [8, 4096, 1536], P('dp', 'seq'), may hold values from -6 to 6
- upstream: bfloat16 [8, 4096, 1536], P('dp', 'seq'), may hold values from -6 to 6
- utt_span: int32 [2, 8, 4096], P(None, 'dp', 'seq'), may hold values from 0 to 4096, as said below
- w_qkv: bfloat16 [1536, 2304], P('dp')
- w_out: bfloat16 [768, 1536], P('dp'), may hold values from -0.21875 to 0.21875
Outputs:
- branch: bfloat16 [8, 4096, 1536], P('dp', 'seq')
- grad_in: bfloat16 [8, 4096, 1536], P('dp', 'seq')
- grad_qkv: float32 [1536, 2304], P(('dp', 'seq'))
- grad_out: float32 [768, 1536], P(('dp', 'seq'))
The draws below stay inside these ranges and needn't reach their ends.
Inputs may be any that keep to these rules, and one draw needn't show every extreme that they name: In each row the utterances tile the frames: for frame i, utt_span[0] <= i < utt_span[1], and all frames of an utterance carry the same pair.
All inputs are finite; a program needn't handle non-finite values.
Results may differ from the reference program's by a relative error of at most 0.015.
Values may be sent and summed in bfloat16 or wider, within the bound.
No kernel may reach another device: no remote copies, remote signals or barrier semaphores. Data moves between devices by JAX's collectives and lax.ppermute only.
A program may use at most 128 MiB of HBM per device.

```python
import jax
import jax.numpy as jnp
from jax import lax

D = 1536
HEADS = 12
HEAD_DIM = 64
STRETCH = 64
PRIOR = 4
BATCH = 8
LENGTH = 4096
INNER = 768


def draw_utt_span(key, part):
    marks = jax.random.randint(key, (BATCH, LENGTH), 0, 10 * STRETCH)
    position = jnp.arange(LENGTH, dtype=jnp.int32)[None, :]
    is_first = (marks == 0) | (position == 0)
    starts = lax.cummax(jnp.where(is_first, position, 0), axis=1)
    next_first = jnp.where(is_first, position, LENGTH)
    shifted = jnp.concatenate([next_first[:, 1:], jnp.full((BATCH, 1), LENGTH, jnp.int32)], axis=1)
    limits = lax.cummin(shifted, axis=1, reverse=True)
    return jnp.stack([starts, limits]).astype(jnp.int32)


def draw_w_qkv(key, part):
    seed_base = jax.random.fold_in(key, 0)
    inner_cols = HEADS * HEAD_DIM
    matrix = jax.random.normal(seed_base, (D, 3 * inner_cols), jnp.float32) * D ** (-0.5)
    return matrix.astype(jnp.bfloat16)


def level_of(stream_key, extent, cuts, smallest, high):
    level, own = 1.0, jax.random.fold_in(stream_key, 6)
    for axis_at, parts in cuts:
        heights = jnp.exp(jax.random.uniform(jax.random.fold_in(own, axis_at), (parts,), jnp.float32, smallest / len(cuts), high / len(cuts)))
        level = level * jnp.repeat(heights, extent[axis_at] // parts).reshape([-1 if axis == axis_at else 1 for axis in range(len(extent))])
    return level


def noise(own_key, shape, scale, most, cuts=(), held_as=jnp.bfloat16):
    drawn = scale * jax.random.normal(own_key, shape, jnp.float32)
    if cuts:
        drawn = drawn * level_of(own_key, shape, cuts, -0.22, 0.18)
    return jnp.clip(drawn, -most, most).astype(held_as)


def setup_inputs(seed: int = 0) -> dict:
    keys = jax.random.split(jax.random.key(seed), 6)
    return {
        "frames": noise(keys[0], (BATCH, LENGTH, D), 1.0, 6.0, ((0, 8), (1, 16))),
        "upstream": noise(keys[1], (BATCH, LENGTH, D), 1.0, 6.0, ((0, 8), (1, 16))),
        "utt_span": draw_utt_span(jax.random.fold_in(keys[5], 71), 0),
        "w_qkv": draw_w_qkv(jax.random.fold_in(keys[5], 71), 0),
        "w_out": noise(keys[4], (INNER, D), INNER ** -0.5, 0.21875, ((0, 8),)),
    }


EPS = 1e-05

def normalize(inputs):
    widened = inputs.astype(jnp.float32)
    centered = widened - lax.optimization_barrier(jnp.mean(widened, axis=-1, keepdims=True))
    inv_sigma = lax.rsqrt(lax.optimization_barrier(jnp.mean(centered * centered, axis=-1, keepdims=True)) + EPS)
    return (centered * inv_sigma, inv_sigma)

def contract(form, left, right):
    return jnp.einsum(form, left.astype(jnp.float32), right.astype(jnp.float32), precision=lax.Precision.HIGHEST)

def windows(extended):
    stretch_total = extended.shape[0] // STRETCH
    stretch_count = stretch_total - PRIOR
    blocked = extended.reshape((stretch_total, STRETCH) + extended.shape[1:])
    return jnp.concatenate([blocked[shift_by:shift_by + stretch_count] for shift_by in range(PRIOR + 1)], axis=1)

def unwindow(windowed):
    stretch_count = windowed.shape[0]
    parted = windowed.reshape((stretch_count, PRIOR + 1, STRETCH) + windowed.shape[2:])
    running = jnp.zeros((stretch_count + PRIOR, STRETCH) + windowed.shape[2:], jnp.float32)
    for shift_by in range(PRIOR + 1):
        running = running.at[shift_by:shift_by + stretch_count].add(parted[:, shift_by])
    return running.reshape(((stretch_count + PRIOR) * STRETCH,) + windowed.shape[2:])

def visible(starts, limits, offset):
    stretch_count = starts.shape[0] // STRETCH
    block_first = jnp.arange(stretch_count, dtype=jnp.int32)[:, None] * STRETCH
    key_pos = offset - PRIOR * STRETCH + block_first + jnp.arange((PRIOR + 1) * STRETCH, dtype=jnp.int32)[None, :]
    lowest = starts.reshape(stretch_count, STRETCH)
    beyond = limits.reshape(stretch_count, STRETCH)
    return (key_pos[:, None, :] >= lowest[:, :, None]) & (key_pos[:, None, :] < beyond[:, :, None])

def attend_forward(queries, keys_ext, values_ext, mask):
    stretch_count = queries.shape[0] // STRETCH
    query_blocks = queries.reshape(stretch_count, STRETCH, HEADS, HEAD_DIM)
    key_windows = windows(keys_ext.reshape(-1, HEADS, HEAD_DIM))
    value_windows = windows(values_ext.reshape(-1, HEADS, HEAD_DIM))
    scores = contract('nqhd,nkhd->nhqk', query_blocks, key_windows) * HEAD_DIM ** (-0.5)
    allowed = mask[:, None]
    masked = jnp.where(allowed, scores, -1e+30)
    highest = lax.optimization_barrier(jnp.max(masked, axis=-1, keepdims=True))
    weights = jnp.where(allowed, jnp.exp(masked - highest), 0.0)
    probs = weights / lax.optimization_barrier(jnp.sum(weights, axis=-1, keepdims=True))
    probs_low = probs.astype(jnp.bfloat16)
    context = contract('nhqk,nkhd->nqhd', probs_low, value_windows).astype(jnp.bfloat16)
    return (context.reshape(queries.shape), (query_blocks, key_windows, value_windows, probs, probs_low))

def attend_backward(saved, d_context):
    query_blocks, key_windows, value_windows, probs, probs_low = saved
    d_blocks = d_context.reshape(query_blocks.shape)
    d_probs = contract('nqhd,nkhd->nhqk', d_blocks, value_windows)
    d_scores = probs * (d_probs - lax.optimization_barrier(jnp.sum(probs * d_probs, axis=-1, keepdims=True)))
    d_scores_low = (d_scores * HEAD_DIM ** (-0.5)).astype(jnp.bfloat16)
    d_queries = contract('nhqk,nkhd->nqhd', d_scores_low, key_windows).astype(jnp.bfloat16)
    d_keys = unwindow(contract('nhqk,nqhd->nkhd', d_scores_low, query_blocks))
    d_values = unwindow(contract('nhqk,nqhd->nkhd', probs_low, d_blocks))
    ext_rows = d_keys.shape[0]
    return (d_queries.reshape(d_context.shape), d_keys.reshape(ext_rows, -1), d_values.reshape(ext_rows, -1))

def reference(frames, upstream, utt_span, w_qkv, w_out):
    inner_width = HEADS * HEAD_DIM
    halo_rows = PRIOR * STRETCH

    def one_row(carry, row_inputs):
        own_frames, own_grad, starts, limits = row_inputs
        normed, inv_sigma = normalize(own_frames)
        normed_low = normed.astype(jnp.bfloat16)
        projected = jnp.dot(normed_low, w_qkv, preferred_element_type=jnp.float32).astype(jnp.bfloat16)
        queries = projected[:, :inner_width]
        keys_all = projected[:, inner_width:2 * inner_width]
        values_all = projected[:, 2 * inner_width:]
        padding = jnp.zeros((halo_rows, inner_width), jnp.bfloat16)
        keys_ext = jnp.concatenate([padding, keys_all], axis=0)
        values_ext = jnp.concatenate([padding, values_all], axis=0)
        context, saved = attend_forward(queries, keys_ext, values_ext, visible(starts, limits, 0))
        branch = jnp.dot(context, w_out, preferred_element_type=jnp.float32).astype(jnp.bfloat16)
        d_context = jnp.dot(own_grad, w_out.T, preferred_element_type=jnp.float32).astype(jnp.bfloat16)
        d_queries, d_keys, d_values = attend_backward(saved, d_context)
        d_proj = jnp.concatenate([d_queries, d_keys[halo_rows:].astype(jnp.bfloat16), d_values[halo_rows:].astype(jnp.bfloat16)], axis=1)
        grad_qkv = carry[0] + jnp.dot(normed_low.T, d_proj, preferred_element_type=jnp.float32)
        grad_out = carry[1] + jnp.dot(context.T, own_grad, preferred_element_type=jnp.float32)
        d_normed = jnp.dot(d_proj, w_qkv.T, preferred_element_type=jnp.float32)
        grad_in = inv_sigma * (d_normed - lax.optimization_barrier(jnp.mean(d_normed, axis=-1, keepdims=True)) - normed * lax.optimization_barrier(jnp.mean(d_normed * normed, axis=-1, keepdims=True)))
        return ((grad_qkv, grad_out), (branch, grad_in.astype(jnp.bfloat16)))
    initial = (jnp.zeros((D, 3 * inner_width), jnp.float32), jnp.zeros((inner_width, D), jnp.float32))
    sums, outputs = lax.scan(one_row, initial, (frames, upstream, utt_span[0], utt_span[1]))
    return (outputs[0], outputs[1], sums[0], sums[1])
```

```python
import functools

import jax
import jax.numpy as jnp
from jax import lax
from jax.experimental import pallas as pl
from jax.experimental.pallas import tpu as pltpu
from jax.sharding import Mesh
from jax.sharding import PartitionSpec as P

HEAD_DIM = 64
STRETCH = 64
PRIOR = 4
WINDOW = (PRIOR + 1) * STRETCH
PAIR = 2 * HEAD_DIM
EPS = 1e-05

BF = jnp.bfloat16
F32 = jnp.float32


def nt(a, b):
    return lax.dot_general(a, b, (((1,), (1,)), ((), ())), preferred_element_type=F32)


def tn(a, b):
    return lax.dot_general(a, b, (((0,), (0,)), ((), ())), preferred_element_type=F32)


def nn(a, b):
    return lax.dot_general(a, b, (((1,), (0,)), ((), ())), preferred_element_type=F32)


def attend(first, lo_ref, hi_ref, proj_ref, dctx_ref, ctx_ref, dq_ref, dk_ref, dv_ref):
    width = ctx_ref.shape[1]
    blocks = ctx_ref.shape[0] // STRETCH
    dk_ref[...] = jnp.zeros_like(dk_ref)
    dv_ref[...] = jnp.zeros_like(dv_ref)
    lanes = lax.broadcasted_iota(jnp.int32, (STRETCH, PAIR), 1) < HEAD_DIM
    key_at = lax.broadcasted_iota(jnp.int32, (WINDOW, PAIR), 0)

    def stack(value):
        none = jnp.zeros_like(value)
        return jnp.concatenate(
            [jnp.where(lanes, value, none), jnp.where(lanes, none, value)], axis=0
        )

    def unstack(value):
        return jnp.where(lanes, value[:STRETCH], value[STRETCH:])

    for b in range(blocks):
        rows = pl.ds(b * STRETCH, STRETCH)
        seen = (key_at >= lo_ref[b : b + 1, :]) & (key_at < hi_ref[b : b + 1, :])
        for pair in range(width // PAIR):
            cols = pl.ds(pair * PAIR, PAIR)
            window = pl.ds(b * STRETCH, WINDOW)
            queries = stack(
                proj_ref[pl.ds(first + PRIOR * STRETCH + b * STRETCH, STRETCH), cols]
            )
            source = pl.ds(first + b * STRETCH, WINDOW)
            keys = proj_ref[source, pl.ds(width + pair * PAIR, PAIR)]
            values = proj_ref[source, pl.ds(2 * width + pair * PAIR, PAIR)]
            d_out = stack(dctx_ref[rows, cols])
            scores = jnp.where(seen, nt(keys, queries) * HEAD_DIM ** (-0.5), -1e30)
            weights = jnp.exp(scores - jnp.max(scores, axis=0, keepdims=True))
            probs = weights * (1.0 / jnp.sum(weights, axis=0, keepdims=True))
            low = probs.astype(BF)
            d_probs = nt(values, d_out)
            centre = jnp.sum(probs * d_probs, axis=0, keepdims=True)
            d_scores = (probs * (d_probs - centre) * HEAD_DIM ** (-0.5)).astype(BF)
            ctx_ref[rows, cols] = unstack(tn(low, values)).astype(BF)
            dq_ref[rows, cols] = unstack(tn(d_scores, keys)).astype(BF)
            dk_ref[window, cols] += nn(d_scores, queries)
            dv_ref[window, cols] += nn(low, d_out)


def attention(first, lo, hi, proj, d_context):
    queries, width = d_context.shape
    ext = queries + PRIOR * STRETCH
    whole = pl.BlockSpec(memory_space=pltpu.VMEM)
    return pl.pallas_call(
        functools.partial(attend, first),
        in_specs=[whole] * 4,
        out_specs=[whole] * 4,
        out_shape=[
            jax.ShapeDtypeStruct((queries, width), BF),
            jax.ShapeDtypeStruct((queries, width), BF),
            jax.ShapeDtypeStruct((ext, width), F32),
            jax.ShapeDtypeStruct((ext, width), F32),
        ],
        compiler_params=pltpu.CompilerParams(vmem_limit_bytes=40 * 1024 * 1024),
        name="attend",
    )(lo, hi, proj, d_context)


def normalize(inputs):
    widened = inputs.astype(F32)
    centered = widened - jnp.mean(widened, axis=-1, keepdims=True)
    inv_sigma = lax.rsqrt(jnp.mean(centered * centered, axis=-1, keepdims=True) + EPS)
    return (centered * inv_sigma, inv_sigma)


DP, CHIPS, CORES = 8, 8, 2
ALL = ("dp", "t", "c")


def device(dp, t, c):
    return (dp * CHIPS + t) * CORES + c


EVERY = [(d, t, c) for d in range(DP) for t in range(CHIPS) for c in range(CORES)]
SWAP = [(device(d, t, c), device(d, t, 1 - c)) for d, t, c in EVERY]
ONWARD = [(device(d, t, c), device(d, t + 1, c)) for d, t, c in EVERY if t + 1 < CHIPS]
BACK = [(device(d, t, c), device(d, t - 1, c)) for d, t, c in EVERY if t > 0]
OWNER = [(device(d, t, c), c * DP * CHIPS + d * CHIPS + t) for d, t, c in EVERY]


def swap(value):
    return lax.ppermute(value, ALL, SWAP)


def spread(grad):
    rows, columns = grad.shape
    third = columns // 4
    to = lax.broadcasted_iota(jnp.int32, (rows // 6 * 8, rows), 0)
    at = lax.broadcasted_iota(jnp.int32, (rows // 6 * 8, rows), 1)
    base = to // 8 * 6
    slot = to % 8
    keep = ((slot < 6) & (at == base + slot)).astype(BF)
    parts = []
    for b in range(3):
        tail = (((slot == 6) & (at == base + b)) | ((slot == 7) & (at == base + 3 + b))).astype(BF)
        parts.append(nn(keep, grad[:, b * third : (b + 1) * third]) + nn(tail, grad[:, 3 * third :]))
    return jnp.concatenate(parts, axis=1).astype(BF)


def gather(shard):
    copies = jnp.broadcast_to(shard[None], (DP,) + shard.shape)
    return lax.all_to_all(copies, "dp", 0, 0, tiled=True)


def body(frames, upstream, utt_span, w_qkv, w_out):
    core = lax.axis_index("c")
    lower = core == 0
    own_frames = frames[0]
    own_grad = upstream[0]
    count, wide = own_frames.shape
    inner = w_qkv.shape[1] // 3
    width = inner // CORES
    halo = PRIOR * STRETCH

    def both(own):
        other = swap(own)
        return jnp.concatenate(
            [jnp.where(lower, own, other), jnp.where(lower, other, own)], axis=0
        )

    normed, inv_sigma = normalize(own_frames)
    own_low = normed.astype(BF)
    low = both(own_low)
    history = lax.ppermute(low[count:], ALL, ONWARD)
    low_ext = jnp.concatenate([history, low], axis=0)
    grad_all = both(own_grad)

    spans = jnp.swapaxes(utt_span[:, 0], 0, 1)
    spans = both(spans).T - lax.axis_index("t") * (CORES * count) + halo
    blocked = spans.reshape(2, -1, STRETCH)
    blocked = blocked - (jnp.arange(blocked.shape[1], dtype=jnp.int32) * STRETCH)[None, :, None]
    blocked = jnp.concatenate([blocked, blocked], axis=-1)
    half = blocked.shape[1] // 2

    mine = lax.dynamic_index_in_dim(
        w_qkv.reshape(-1, 3, CORES, width), core, axis=2, keepdims=False
    ).reshape(-1, 3 * width)
    full_qkv = gather(mine).reshape(wide, 3 * width)
    out_cols = wide // CORES
    out_mine = gather(
        lax.dynamic_slice_in_dim(w_out, core * out_cols, out_cols, axis=1)
    ).reshape(inner, out_cols)
    out_kept = lax.dynamic_slice_in_dim(out_mine, core * width, width, axis=0)
    out_other = swap(lax.dynamic_slice_in_dim(out_mine, (1 - core) * width, width, axis=0))
    full_out = jnp.concatenate(
        [jnp.where(lower, out_kept, out_other), jnp.where(lower, out_other, out_kept)], axis=1
    )

    projected = nn(low_ext, full_qkv).astype(BF)
    d_context = nt(grad_all, full_out).astype(BF)

    ctx_a, dq_a, dk_a, dv_a = attention(
        0, blocked[0, :half], blocked[1, :half], projected, d_context[:count]
    )
    returned = lax.ppermute(
        jnp.concatenate([dk_a[:halo], dv_a[:halo]], axis=1).astype(BF), ALL, BACK
    ).astype(F32)
    ctx_b, dq_b, dk_b, dv_b = attention(
        count, blocked[0, half:], blocked[1, half:], projected, d_context[count:]
    )
    context = jnp.concatenate([ctx_a, ctx_b], axis=0)
    partial = nn(context, full_out)
    kept = lax.dynamic_slice_in_dim(partial, core * count, count, axis=0)
    other = swap(lax.dynamic_slice_in_dim(partial, (1 - core) * count, count, axis=0).astype(BF))
    branch = (kept + other.astype(F32)).astype(BF)

    d_low = jnp.concatenate([dk_a[halo:] + dk_b[:halo], dv_a[halo:] + dv_b[:halo]], axis=1)
    d_high = jnp.concatenate([dk_b[halo:], dv_b[halo:]], axis=1) + returned
    d_proj = jnp.concatenate(
        [
            jnp.concatenate([dq_a, d_low.astype(BF)], axis=1),
            jnp.concatenate([dq_b, d_high.astype(BF)], axis=1),
        ],
        axis=0,
    )
    grad_out = spread(tn(context, grad_all).astype(BF))
    grad_qkv = tn(low, d_proj).astype(BF)
    chips = DP * CHIPS
    sent = jnp.concatenate(
        [grad_qkv.reshape(chips, -1, 3 * width), grad_out.reshape(chips, -1, 3 * width)], axis=1
    )
    arrived = lax.all_to_all(sent, ("dp", "t"), 0, 0, tiled=True)
    total = jnp.sum(arrived.astype(F32), axis=0)
    rows = wide // chips // CORES
    q_total, o_total = total[: CORES * rows], total[CORES * rows :]
    q_kept = lax.dynamic_slice_in_dim(q_total, core * rows, rows, axis=0)
    q_other = swap(lax.dynamic_slice_in_dim(q_total, (1 - core) * rows, rows, axis=0))
    q_kept = q_kept.reshape(rows, 3, 1, width)
    q_other = q_other.reshape(rows, 3, 1, width)
    q_out = jnp.concatenate(
        [jnp.where(lower, q_kept, q_other), jnp.where(lower, q_other, q_kept)], axis=2
    ).reshape(rows, 3 * inner)
    o_rows = inner // chips // CORES
    o_out = jnp.concatenate(
        [o_total[:o_rows], o_total[o_rows:].reshape(o_rows, wide - 3 * width)], axis=1
    )
    o_out = lax.ppermute(o_out, ALL, OWNER)

    d_partial = nt(d_proj, full_qkv)
    d_kept = lax.dynamic_slice_in_dim(d_partial, core * count, count, axis=0)
    d_other = swap(
        lax.dynamic_slice_in_dim(d_partial, (1 - core) * count, count, axis=0).astype(BF)
    )
    d_normed = d_kept + d_other.astype(F32)
    grad_in = inv_sigma * (
        d_normed
        - jnp.mean(d_normed, axis=-1, keepdims=True)
        - normed * jnp.mean(d_normed * normed, axis=-1, keepdims=True)
    )
    return (branch[None], grad_in.astype(BF)[None], q_out, o_out)


def solution(mesh):
    fine = Mesh(mesh.devices.reshape(DP, CHIPS, CORES), ALL)
    rows = P("dp", ("t", "c"), None)
    in_specs = (rows, rows, P(None, "dp", ("t", "c")), P("dp", None), P("dp", None))
    out_specs = (rows, rows, P(ALL, None), P(ALL, None))
    return jax.shard_map(body, mesh=fine, in_specs=in_specs, out_specs=out_specs, check_vma=False)
```

```python
import functools

import jax
import jax.numpy as jnp
from jax import lax
from jax.experimental import pallas as pl
from jax.experimental.pallas import tpu as pltpu
from jax.sharding import Mesh
from jax.sharding import PartitionSpec as P

HEAD_DIM = 64
STRETCH = 64
PRIOR = 4
WINDOW = (PRIOR + 1) * STRETCH
PAIR = 2 * HEAD_DIM
EPS = 1e-05

BF = jnp.bfloat16
F32 = jnp.float32


def nt(a, b):
    return lax.dot_general(a, b, (((1,), (1,)), ((), ())), preferred_element_type=F32)


def tn(a, b):
    return lax.dot_general(a, b, (((0,), (0,)), ((), ())), preferred_element_type=F32)


def nn(a, b):
    return lax.dot_general(a, b, (((1,), (0,)), ((), ())), preferred_element_type=F32)


def attend(first, lo_ref, hi_ref, proj_ref, dctx_ref, ctx_ref, dq_ref, dk_ref, dv_ref):
    width = ctx_ref.shape[1]
    blocks = ctx_ref.shape[0] // STRETCH
    dk_ref[...] = jnp.zeros_like(dk_ref)
    dv_ref[...] = jnp.zeros_like(dv_ref)
    lanes = lax.broadcasted_iota(jnp.int32, (STRETCH, PAIR), 1) < HEAD_DIM
    key_at = lax.broadcasted_iota(jnp.int32, (WINDOW, PAIR), 0)

    def stack(value):
        none = jnp.zeros_like(value)
        return jnp.concatenate(
            [jnp.where(lanes, value, none), jnp.where(lanes, none, value)], axis=0
        )

    def unstack(value):
        return jnp.where(lanes, value[:STRETCH], value[STRETCH:])

    for b in range(blocks):
        rows = pl.ds(b * STRETCH, STRETCH)
        seen = (key_at >= lo_ref[b : b + 1, :]) & (key_at < hi_ref[b : b + 1, :])
        for pair in range(width // PAIR):
            cols = pl.ds(pair * PAIR, PAIR)
            window = pl.ds(b * STRETCH, WINDOW)
            queries = stack(
                proj_ref[pl.ds(first + PRIOR * STRETCH + b * STRETCH, STRETCH), cols]
            )
            source = pl.ds(first + b * STRETCH, WINDOW)
            keys = proj_ref[source, pl.ds(width + pair * PAIR, PAIR)]
            values = proj_ref[source, pl.ds(2 * width + pair * PAIR, PAIR)]
            d_out = stack(dctx_ref[rows, cols])
            scores = jnp.where(seen, nt(keys, queries) * HEAD_DIM ** (-0.5), -1e30)
            weights = jnp.exp(scores - jnp.max(scores, axis=0, keepdims=True))
            probs = weights * (1.0 / jnp.sum(weights, axis=0, keepdims=True))
            low = probs.astype(BF)
            d_probs = nt(values, d_out)
            centre = jnp.sum(probs * d_probs, axis=0, keepdims=True)
            d_scores = (probs * (d_probs - centre) * HEAD_DIM ** (-0.5)).astype(BF)
            ctx_ref[rows, cols] = unstack(tn(low, values)).astype(BF)
            dq_ref[rows, cols] = unstack(tn(d_scores, keys)).astype(BF)
            dk_ref[window, cols] += nn(d_scores, queries)
            dv_ref[window, cols] += nn(low, d_out)


def attention(first, lo, hi, proj, d_context):
    queries, width = d_context.shape
    ext = queries + PRIOR * STRETCH
    whole = pl.BlockSpec(memory_space=pltpu.VMEM)
    return pl.pallas_call(
        functools.partial(attend, first),
        in_specs=[whole] * 4,
        out_specs=[whole] * 4,
        out_shape=[
            jax.ShapeDtypeStruct((queries, width), BF),
            jax.ShapeDtypeStruct((queries, width), BF),
            jax.ShapeDtypeStruct((ext, width), F32),
            jax.ShapeDtypeStruct((ext, width), F32),
        ],
        compiler_params=pltpu.CompilerParams(vmem_limit_bytes=40 * 1024 * 1024),
        name="attend",
    )(lo, hi, proj, d_context)


def normalize(inputs):
    widened = inputs.astype(F32)
    centered = widened - jnp.mean(widened, axis=-1, keepdims=True)
    inv_sigma = lax.rsqrt(jnp.mean(centered * centered, axis=-1, keepdims=True) + EPS)
    return (centered * inv_sigma, inv_sigma)


SIZES = {"z": 4, "xl": 2, "y": 4, "xh": 2, "c": 2}
ALL = tuple(SIZES)
DP, CHIPS, CORES, ROWS_Y = 8, 8, 2, 4


def device(dp, t, c):
    return (dp * CHIPS + t) * CORES + c


EVERY = [(d, t, c) for d in range(DP) for t in range(CHIPS) for c in range(CORES)]
SWAP = [(device(d, t, c), device(d, t, 1 - c)) for d, t, c in EVERY]
ONWARD = [(device(d, t, 1), device(d, t + 1, 1)) for d, t, c in EVERY if c and t + 1 < CHIPS]
BACK = [(device(d, t, c), device(d, t - 1, c)) for d, t, c in EVERY if t > 0]
OWNER = [(device(d, t, c), c * DP * CHIPS + d * CHIPS + t) for d, t, c in EVERY]


def from_y(by):
    return [(device(d, (t + 2 * by) % CHIPS, c), device(d, t, c)) for d, t, c in EVERY]


def swap(value):
    return lax.ppermute(value, ALL, SWAP)


def gradients(
    ctx_a, ctx_b, up_ref, low_ref, dq_a, dq_b, dk_a, dk_b, dv_a, dv_b, first_ref, late_ref, out_scr, d_ref
):
    step = pl.program_id(0)

    @pl.when(step == 0)
    def _():
        count, width = ctx_a.shape
        out_scr[...] = (
            tn(ctx_a[...], up_ref[:count, :]) + tn(ctx_b[...], up_ref[count:, :])
        ).astype(BF)
        halo = d_ref.shape[0] - 2 * count
        d_ref[:halo, :width] = jnp.zeros((halo, width), BF)
        d_ref[halo : halo + count, :width] = dq_a[...]
        d_ref[halo + count :, :width] = dq_b[...]
        for at, early, late in ((width, dk_a, dk_b), (2 * width, dv_a, dv_b)):
            cols = slice(at, at + width)
            d_ref[:halo, cols] = early[:halo, :].astype(BF)
            d_ref[halo : halo + count, cols] = (early[halo:, :] + late[:halo, :]).astype(BF)
            d_ref[halo + count :, cols] = late[halo:, :].astype(BF)

    own = 2 * CHIPS
    columns = d_ref.shape[1]
    third = columns // 3
    to = lax.broadcasted_iota(jnp.int32, (own * 8, own * 6), 0)
    at = lax.broadcasted_iota(jnp.int32, (own * 8, own * 6), 1)
    base, slot = to // 8 * 6, to % 8
    keep = ((slot < 6) & (at == base + slot)).astype(BF)
    rows = out_scr[pl.ds(pl.multiple_of(step * own * 6, 32), own * 6), :]
    parts = []
    for b in range(3):
        tail = (((slot == 6) & (at == base + b)) | ((slot == 7) & (at == base + 3 + b))).astype(BF)
        parts.append(
            nn(keep, rows[:, b * third : (b + 1) * third]) + nn(tail, rows[:, 3 * third :])
        )
    folded = jnp.concatenate(parts, axis=1)
    grad = tn(low_ref[...], d_ref[...])
    for j in range(own):
        dp, y, xh = j // CHIPS, j % CHIPS // 2, j % 2
        late_ref[dp, xh, y] = grad[j * 24 : j * 24 + 16].astype(BF)
        first_ref[y, dp, xh] = jnp.concatenate(
            [grad[j * 24 + 16 : j * 24 + 24], folded[j * 8 : j * 8 + 8]], axis=0
        ).astype(BF)


def weight_gradients(grad_all, low_ext, contexts, d_queries, d_keys, d_values):
    wide = grad_all.shape[1]
    width = contexts[0].shape[1]
    ext, columns = low_ext.shape[0], 3 * width
    steps = DP // 2
    parts = (*d_queries, *d_keys, *d_values)

    def whole(value):
        return pl.BlockSpec(value.shape, lambda i: (0, 0))

    return pl.pallas_call(
        gradients,
        grid=(steps,),
        in_specs=[
            whole(contexts[0]),
            whole(contexts[1]),
            whole(grad_all),
            pl.BlockSpec((ext, wide // steps), lambda i: (0, i)),
            *[whole(part) for part in parts],
        ],
        out_specs=[
            pl.BlockSpec((ROWS_Y, 2, 2, 16, columns), lambda i: (0, i, 0, 0, 0)),
            pl.BlockSpec((2, 2, ROWS_Y, 16, columns), lambda i: (i, 0, 0, 0, 0)),
        ],
        out_shape=[
            jax.ShapeDtypeStruct((ROWS_Y, DP, 2, 16, columns), BF),
            jax.ShapeDtypeStruct((DP, 2, ROWS_Y, 16, columns), BF),
        ],
        scratch_shapes=[pltpu.VMEM((width, wide), BF), pltpu.VMEM((ext, columns), BF)],
        compiler_params=pltpu.CompilerParams(vmem_limit_bytes=48 * 1024 * 1024),
        name="weight_gradients",
    )(*contexts, grad_all, low_ext, *parts)


def own_half(core, value, size, axis=0):
    return lax.dynamic_slice_in_dim(value, core * size, size, axis=axis)


def other_half(core, value, size, axis=0):
    return lax.dynamic_slice_in_dim(value, (1 - core) * size, size, axis=axis)


def in_order(lower, own, other, axis):
    return jnp.concatenate(
        [jnp.where(lower, own, other), jnp.where(lower, other, own)], axis=axis
    )


def scatter(chunks):
    return lax.all_to_all(chunks, ("z", "xl", "xh"), 0, 0, tiled=True)


def gather(shard):
    copies = jnp.broadcast_to(shard[None], (DP,) + shard.shape)
    return lax.all_to_all(copies, ("z", "xl"), 0, 0, tiled=True)


def body(frames, upstream, utt_span, w_qkv, w_out):
    core = lax.axis_index("c")
    lower = core == 0
    own_frames = frames[0]
    own_grad = upstream[0]
    count, wide = own_frames.shape
    inner = w_qkv.shape[1] // 3
    width = inner // CORES
    halo = PRIOR * STRETCH
    chips = DP * CHIPS
    out_cols = wide // CORES

    def both(own):
        return in_order(lower, own, swap(own), 0)

    y = lax.axis_index("y")
    mine = own_half(core, w_qkv.reshape(-1, 3, inner), width, axis=2).reshape(-1, 3 * width)
    out_mine = own_half(core, w_out, out_cols, axis=1)
    deep = mine.shape[0]
    direct = deep * 2 // 3
    low_rows = deep // 3
    tail = out_mine[low_rows:]
    folded = jnp.concatenate(
        [out_mine[:low_rows], jnp.concatenate([tail[:, :width], tail[:, width:]], axis=0)],
        axis=1,
    )
    indirect = jnp.concatenate(
        [
            mine[direct:].reshape(ROWS_Y, -1, 3 * width),
            folded.reshape(ROWS_Y, -1, 3 * width),
        ],
        axis=1,
    )
    quarter = gather(lax.dynamic_index_in_dim(indirect, y, axis=0, keepdims=False))
    shard, quarter = lax.optimization_barrier((mine[:direct], quarter))
    full_direct = gather(shard)
    quarters = jnp.zeros((ROWS_Y,) + quarter.shape, BF)
    for k in range(ROWS_Y):
        got = quarter if k == 0 else lax.ppermute(quarter, ALL, from_y(k))
        quarters = lax.dynamic_update_index_in_dim(quarters, got, (y + k) % ROWS_Y, 0)
    qkv_rows = (deep - direct) // ROWS_Y
    full_qkv = jnp.concatenate(
        [full_direct] + [quarters[i, :, :qkv_rows] for i in range(ROWS_Y)], axis=1
    ).reshape(wide, 3 * width)
    unfolded = jnp.concatenate([quarters[i, :, qkv_rows:] for i in range(ROWS_Y)], axis=1)
    rest = unfolded[:, :, out_cols:]
    half = rest.shape[1] // 2
    out_half = jnp.concatenate(
        [
            unfolded[:, :, :out_cols],
            jnp.concatenate([rest[:, :half], rest[:, half:]], axis=2),
        ],
        axis=1,
    ).reshape(inner, out_cols)
    full_out = in_order(
        lower,
        own_half(core, out_half, width),
        swap(other_half(core, out_half, width)),
        1,
    )

    normed, inv_sigma = normalize(own_frames)
    own_low = normed.astype(BF)
    low = both(own_low)
    past = lax.ppermute(own_low, ALL, ONWARD)
    low_ext = jnp.concatenate([jnp.where(lower, swap(past), past), low], axis=0)
    grad_all = both(own_grad)

    spans = jnp.swapaxes(utt_span[:, 0], 0, 1)
    spans = both(spans).T - (y * 2 + lax.axis_index("xh")) * (CORES * count) + halo
    blocked = spans.reshape(2, -1, STRETCH)
    blocked = blocked - (jnp.arange(blocked.shape[1], dtype=jnp.int32) * STRETCH)[None, :, None]
    blocked = jnp.concatenate([blocked, blocked], axis=-1)
    middle = blocked.shape[1] // 2

    d_context = nt(grad_all, full_out).astype(BF)
    projected = nn(low_ext, full_qkv).astype(BF)
    ctx_a, dq_a, dk_a, dv_a = attention(
        0, blocked[0, :middle], blocked[1, :middle], projected, d_context[:count]
    )
    d_history = jnp.concatenate([dk_a[:halo], dv_a[:halo]], axis=1).astype(BF)
    returned = lax.ppermute(d_history, ALL, BACK)
    ctx_b, dq_b, dk_b, dv_b = attention(
        count, blocked[0, middle:], blocked[1, middle:], projected, d_context[count:]
    )
    context = jnp.concatenate([ctx_a, ctx_b], axis=0)

    d_low = jnp.concatenate([dk_a[halo:] + dk_b[:halo], dv_a[halo:] + dv_b[:halo]], axis=1)
    d_low = jnp.concatenate([dq_a, d_low.astype(BF)], axis=1)
    d_last = jnp.concatenate([dk_b[halo:], dv_b[halo:]], axis=1)
    first, late = weight_gradients(
        grad_all, low_ext, (ctx_a, ctx_b), (dq_a, dq_b), (dk_a, dk_b), (dv_a, dv_b)
    )
    first, late, returned = lax.optimization_barrier((first, late, returned))
    summed = lax.dynamic_index_in_dim(first, y, axis=0, keepdims=False).astype(F32)
    for k in range(1, ROWS_Y):
        away = lax.dynamic_index_in_dim(first, (y + k) % ROWS_Y, axis=0, keepdims=False)
        summed = summed + lax.ppermute(away, ALL, from_y(-k)).astype(F32)
    summed = summed.astype(BF).reshape(chips // ROWS_Y, 16, 3 * width)
    arrived = scatter(late.reshape(chips // ROWS_Y, ROWS_Y * 16, 3 * width))
    summed, arrived = lax.optimization_barrier((summed, arrived))
    planes = jnp.sum(arrived.astype(F32), axis=0).reshape(ROWS_Y, 16, 3 * width)
    total_late = lax.dynamic_index_in_dim(planes, y, axis=0, keepdims=False)
    for k in range(1, ROWS_Y):
        away = lax.dynamic_index_in_dim(planes, (y + k) % ROWS_Y, axis=0, keepdims=False)
        total_late = total_late + lax.ppermute(away, ALL, from_y(-k))
    total_first = jnp.sum(scatter(summed).astype(F32), axis=0)
    total = jnp.concatenate([total_late, total_first], axis=0)
    d_proj = jnp.concatenate(
        [d_low, jnp.concatenate([dq_b, (d_last + returned.astype(F32)).astype(BF)], axis=1)], axis=0
    )

    o_total = total[CORES * (wide // chips // CORES) :]
    o_rows = inner // chips // CORES
    o_out = jnp.concatenate(
        [o_total[:o_rows], o_total[o_rows:].reshape(o_rows, wide - 3 * width)], axis=1
    )
    o_out = lax.ppermute(o_out, ALL, OWNER)

    rows = wide // chips // CORES
    total = total[: CORES * rows]
    q_kept = own_half(core, total, rows).reshape(rows, 3, width)
    q_other = swap(other_half(core, total, rows)).reshape(rows, 3, width)
    q_out = in_order(lower, q_kept, q_other, 2).reshape(rows, 3 * inner)

    partial = nn(context, full_out)
    branch = (
        own_half(core, partial, count)
        + swap(other_half(core, partial, count).astype(BF)).astype(F32)
    ).astype(BF)

    d_partial = nt(d_proj, full_qkv)
    d_normed = own_half(core, d_partial, count) + swap(
        other_half(core, d_partial, count).astype(BF)
    ).astype(F32)
    grad_in = inv_sigma * (
        d_normed
        - jnp.mean(d_normed, axis=-1, keepdims=True)
        - normed * jnp.mean(d_normed * normed, axis=-1, keepdims=True)
    )
    return (branch[None], grad_in.astype(BF)[None], q_out, o_out)


def solution(mesh):
    fine = Mesh(mesh.devices.reshape(tuple(SIZES.values())), ALL)
    dp, seq = ("z", "xl"), ("y", "xh", "c")
    rows = P(dp, seq, None)
    in_specs = (rows, rows, P(None, dp, seq), P(dp, None), P(dp, None))
    out_specs = (rows, rows, P(ALL, None), P(ALL, None))
    return jax.shard_map(body, mesh=fine, in_specs=in_specs, out_specs=out_specs, check_vma=False)
```

```python
import functools

import jax
import jax.numpy as jnp
from jax import lax
from jax.experimental import pallas as pl
from jax.experimental.pallas import tpu as pltpu
from jax.sharding import Mesh
from jax.sharding import PartitionSpec as P

HEAD_DIM = 64
STRETCH = 64
PRIOR = 4
WINDOW = (PRIOR + 1) * STRETCH
PAIR = 2 * HEAD_DIM
LEAD = 128
EPS = 1e-05

BF = jnp.bfloat16
F32 = jnp.float32


def nt(a, b):
    return lax.dot_general(a, b, (((1,), (1,)), ((), ())), preferred_element_type=F32)


def tn(a, b):
    return lax.dot_general(a, b, (((0,), (0,)), ((), ())), preferred_element_type=F32)


def nn(a, b):
    return lax.dot_general(a, b, (((1,), (0,)), ((), ())), preferred_element_type=F32)


def attend(first, lo_ref, hi_ref, proj_ref, dctx_ref, ctx_ref, dq_ref, dk_ref, dv_ref):
    width = ctx_ref.shape[1]
    blocks = ctx_ref.shape[0] // STRETCH
    dk_ref[...] = jnp.zeros_like(dk_ref)
    dv_ref[...] = jnp.zeros_like(dv_ref)
    lanes = lax.broadcasted_iota(jnp.int32, (STRETCH, PAIR), 1) < HEAD_DIM
    key_at = lax.broadcasted_iota(jnp.int32, (WINDOW, PAIR), 0)

    def stack(value):
        none = jnp.zeros_like(value)
        return jnp.concatenate(
            [jnp.where(lanes, value, none), jnp.where(lanes, none, value)], axis=0
        )

    def unstack(value):
        return jnp.where(lanes, value[:STRETCH], value[STRETCH:])

    for b in range(blocks):
        rows = pl.ds(b * STRETCH, STRETCH)
        seen = (key_at >= lo_ref[b : b + 1, :]) & (key_at < hi_ref[b : b + 1, :])
        for pair in range(width // PAIR):
            cols = pl.ds(pair * PAIR, PAIR)
            window = pl.ds(b * STRETCH, WINDOW)
            queries = stack(
                proj_ref[pl.ds(first + PRIOR * STRETCH + b * STRETCH, STRETCH), cols]
            )
            source = pl.ds(first + b * STRETCH, WINDOW)
            keys = proj_ref[source, pl.ds(width + pair * PAIR, PAIR)]
            values = proj_ref[source, pl.ds(2 * width + pair * PAIR, PAIR)]
            d_out = stack(dctx_ref[rows, cols])
            scores = jnp.where(seen, nt(keys, queries) * HEAD_DIM ** (-0.5), -1e30)
            weights = jnp.exp(scores - jnp.max(scores, axis=0, keepdims=True))
            probs = weights * (1.0 / jnp.sum(weights, axis=0, keepdims=True))
            low = probs.astype(BF)
            d_probs = nt(values, d_out)
            centre = jnp.sum(probs * d_probs, axis=0, keepdims=True)
            d_scores = (probs * (d_probs - centre) * HEAD_DIM ** (-0.5)).astype(BF)
            ctx_ref[rows, cols] = unstack(tn(low, values)).astype(BF)
            dq_ref[rows, cols] = unstack(tn(d_scores, keys)).astype(BF)
            dk_ref[window, cols] += nn(d_scores, queries)
            dv_ref[window, cols] += nn(low, d_out)


def attention(first, lo, hi, proj, d_context):
    queries, width = d_context.shape
    ext = queries + PRIOR * STRETCH
    whole = pl.BlockSpec(memory_space=pltpu.VMEM)
    return pl.pallas_call(
        functools.partial(attend, first),
        in_specs=[whole] * 4,
        out_specs=[whole] * 4,
        out_shape=[
            jax.ShapeDtypeStruct((queries, width), BF),
            jax.ShapeDtypeStruct((queries, width), BF),
            jax.ShapeDtypeStruct((ext, width), F32),
            jax.ShapeDtypeStruct((ext, width), F32),
        ],
        compiler_params=pltpu.CompilerParams(vmem_limit_bytes=40 * 1024 * 1024),
        name="attend",
    )(lo, hi, proj, d_context)


def normalize(inputs):
    widened = inputs.astype(F32)
    centered = widened - jnp.mean(widened, axis=-1, keepdims=True)
    inv_sigma = lax.rsqrt(jnp.mean(centered * centered, axis=-1, keepdims=True) + EPS)
    return (centered * inv_sigma, inv_sigma)


SIZES = {"z": 4, "xl": 2, "y": 4, "xh": 2, "c": 2}
ALL = tuple(SIZES)
DP, CHIPS, CORES, ROWS_Y = 8, 8, 2, 4


def device(dp, t, c):
    return (dp * CHIPS + t) * CORES + c


EVERY = [(d, t, c) for d in range(DP) for t in range(CHIPS) for c in range(CORES)]
SWAP = [(device(d, t, c), device(d, t, 1 - c)) for d, t, c in EVERY]
ONWARD = [(device(d, t, 1), device(d, t + 1, 1)) for d, t, c in EVERY if c and t + 1 < CHIPS]
BACK = [(device(d, t, c), device(d, t - 1, c)) for d, t, c in EVERY if t > 0]


def from_y(by):
    return [(device(d, (t + 2 * by) % CHIPS, c), device(d, t, c)) for d, t, c in EVERY]


def swap(value):
    return lax.ppermute(value, ALL, SWAP)


def fill(d_ref, at, early, late, halo, take):
    count = d_ref.shape[0] - early.shape[0]
    cols = slice(at, at + take.stop - take.start)
    d_ref[:halo, cols] = early[:halo, take].astype(BF)
    d_ref[halo : halo + count, cols] = (early[halo:, take] + late[:halo, take]).astype(BF)
    d_ref[halo + count :, cols] = late[halo:, take].astype(BF)


def late_gradients(low_ref, dq_a, dq_b, dk_a, dk_b, dv_a, dv_b, late_ref, d_ref):
    @pl.when(pl.program_id(0) == 0)
    def _():
        count, width = dq_a.shape
        halo = d_ref.shape[0] - 2 * count
        d_ref[:halo, :width] = jnp.zeros((halo, width), BF)
        d_ref[halo : halo + count, :width] = dq_a[...]
        d_ref[halo + count :, :width] = dq_b[...]
        fill(d_ref, width, dk_a, dk_b, halo, slice(0, width))
        fill(d_ref, 2 * width, dv_a, dv_b, halo, slice(0, LEAD))

    grad = tn(low_ref[...], d_ref[...])
    for j in range(2 * CHIPS):
        dp, y, xh = j // CHIPS, j % CHIPS // 2, j % 2
        late_ref[dp, xh, y] = grad[j * 24 : j * 24 + 24].astype(BF)


def first_gradients(
    y_ref, ctx_ref, up_ref, low_ref, dv_a, dv_b, *rest
):
    outs, (out_scr, d_ref, grad_scr, fold_scr) = rest[:ROWS_Y], rest[ROWS_Y:]
    step = pl.program_id(0)
    width = dv_a.shape[1]

    @pl.when(step == 0)
    def _():
        out_scr[...] = tn(ctx_ref[...], up_ref[...]).astype(BF)
        halo = d_ref.shape[0] - ctx_ref.shape[0]
        fill(d_ref, 0, dv_a, dv_b, halo, slice(LEAD, width))

    own = 2 * CHIPS
    to = lax.broadcasted_iota(jnp.int32, (own * 24, own * 12), 0)
    at = lax.broadcasted_iota(jnp.int32, (own * 24, own * 12), 1)
    base, slot = to // 24 * 12, to % 24
    rows = out_scr[pl.ds(pl.multiple_of(step * own * 12, 64), own * 12), :]
    folded = jnp.zeros((own * 24, width), F32)
    for q in range(2):
        pick = (slot >= q * 12) & (slot < q * 12 + 12) & (at == base + slot - q * 12)
        folded += nn(pick.astype(BF), rows[:, q * width : (q + 1) * width])
    fold_scr[...] = folded
    grad_scr[...] = tn(low_ref[...], d_ref[...])
    for k in range(ROWS_Y):
        y = lax.rem(y_ref[0] + k, ROWS_Y)
        for dp in range(2):
            for xh in range(2):
                chunk = pl.ds(pl.multiple_of(((dp * ROWS_Y + y) * 2 + xh) * 24, 8), 24)
                outs[k][dp, xh] = jnp.concatenate(
                    [grad_scr[chunk, :], fold_scr[chunk, :]], axis=1
                ).astype(BF)


def whole(value):
    return pl.BlockSpec(value.shape, lambda i: (0, 0))


def late_part(low_ext, *parts):
    ext, wide = low_ext.shape
    columns = 2 * parts[0].shape[1] + LEAD
    steps = DP // 2
    return pl.pallas_call(
        late_gradients,
        grid=(steps,),
        in_specs=[
            pl.BlockSpec((ext, wide // steps), lambda i: (0, i)),
            *[whole(part) for part in parts],
        ],
        out_specs=pl.BlockSpec((2, 2, ROWS_Y, 24, columns), lambda i: (i, 0, 0, 0, 0)),
        out_shape=jax.ShapeDtypeStruct((DP, 2, ROWS_Y, 24, columns), BF),
        scratch_shapes=[pltpu.VMEM((ext, columns), BF)],
        compiler_params=pltpu.CompilerParams(vmem_limit_bytes=48 * 1024 * 1024),
        name="late_gradients",
    )(low_ext, *parts)


def first_part(y, context, up_half, low_ext, dv_a, dv_b):
    ext, wide = low_ext.shape
    width = dv_a.shape[1]
    steps = DP // 2
    columns = 2 * width - LEAD
    block = pl.BlockSpec((2, 2, 24, columns), lambda i: (i, 0, 0, 0))
    return pl.pallas_call(
        first_gradients,
        grid=(steps,),
        in_specs=[
            pl.BlockSpec(memory_space=pltpu.SMEM),
            whole(context),
            whole(up_half),
            pl.BlockSpec((ext, wide // steps), lambda i: (0, i)),
            whole(dv_a),
            whole(dv_b),
        ],
        out_specs=[block] * ROWS_Y,
        out_shape=[jax.ShapeDtypeStruct((DP, 2, 24, columns), BF)] * ROWS_Y,
        scratch_shapes=[
            pltpu.VMEM((context.shape[1], up_half.shape[1]), BF),
            pltpu.VMEM((ext, width - LEAD), BF),
            pltpu.VMEM((2 * CHIPS * 24, width - LEAD), F32),
            pltpu.VMEM((2 * CHIPS * 24, width), F32),
        ],
        compiler_params=pltpu.CompilerParams(vmem_limit_bytes=48 * 1024 * 1024),
        name="first_gradients",
    )(y.reshape(1), context, up_half, low_ext, dv_a, dv_b)


def own_half(core, value, size, axis=0):
    return lax.dynamic_slice_in_dim(value, core * size, size, axis=axis)


def other_half(core, value, size, axis=0):
    return lax.dynamic_slice_in_dim(value, (1 - core) * size, size, axis=axis)


def in_order(lower, own, other, axis):
    return jnp.concatenate(
        [jnp.where(lower, own, other), jnp.where(lower, other, own)], axis=axis
    )


def scatter(chunks):
    return lax.all_to_all(chunks, ("z", "xl", "xh"), 0, 0, tiled=True)


def copies(shard):
    return jnp.broadcast_to(shard[None], (DP,) + shard.shape)


def gather(shards):
    return lax.all_to_all(shards, ("z", "xl"), 0, 0, tiled=True)


def body(frames, upstream, utt_span, w_qkv, w_out):
    core = lax.axis_index("c")
    lower = core == 0
    own_frames = frames[0]
    own_grad = upstream[0]
    count, wide = own_frames.shape
    inner = w_qkv.shape[1] // 3
    width = inner // CORES
    halo = PRIOR * STRETCH
    chips = DP * CHIPS
    out_cols = wide // CORES

    def both(own):
        return in_order(lower, own, swap(own), 0)

    y = lax.axis_index("y")
    mine = own_half(core, w_qkv.reshape(-1, 3, inner), width, axis=2).reshape(-1, 3 * width)
    out_mine = own_half(core, w_out, out_cols, axis=1)
    deep = mine.shape[0]
    direct = deep * 2 // 3
    low_rows = deep // 3
    tail = out_mine[low_rows:]
    folded = jnp.concatenate(
        [out_mine[:low_rows], jnp.concatenate([tail[:, :width], tail[:, width:]], axis=0)],
        axis=1,
    )
    indirect = jnp.concatenate(
        [
            mine[direct:].reshape(ROWS_Y, -1, 3 * width),
            folded.reshape(ROWS_Y, -1, 3 * width),
        ],
        axis=1,
    )
    pieces = copies(lax.dynamic_index_in_dim(indirect, y, axis=0, keepdims=False))
    shards = copies(mine[:direct])
    own_frames, own_grad, pieces = lax.optimization_barrier((own_frames, own_grad, pieces))
    normed, inv_sigma = normalize(own_frames)
    own_low = normed.astype(BF)
    own_low, other_low = lax.optimization_barrier((own_low, swap(own_low)))
    low = in_order(lower, own_low, other_low, 0)
    past = lax.ppermute(own_low, ALL, ONWARD)
    quarter = gather(pieces)
    shards, quarter, past = lax.optimization_barrier((shards, quarter, past))
    full_direct = gather(shards)
    quarters = jnp.zeros((ROWS_Y,) + quarter.shape, BF)
    for k in range(ROWS_Y):
        got = quarter if k == 0 else lax.ppermute(quarter, ALL, from_y(k))
        quarters = lax.dynamic_update_index_in_dim(quarters, got, (y + k) % ROWS_Y, 0)
    qkv_rows = (deep - direct) // ROWS_Y
    full_qkv = jnp.concatenate(
        [full_direct] + [quarters[i, :, :qkv_rows] for i in range(ROWS_Y)], axis=1
    ).reshape(wide, 3 * width)
    unfolded = jnp.concatenate([quarters[i, :, qkv_rows:] for i in range(ROWS_Y)], axis=1)
    rest = unfolded[:, :, out_cols:]
    half = rest.shape[1] // 2
    out_half = jnp.concatenate(
        [
            unfolded[:, :, :out_cols],
            jnp.concatenate([rest[:, :half], rest[:, half:]], axis=2),
        ],
        axis=1,
    ).reshape(inner, out_cols)
    full_out = in_order(
        lower,
        own_half(core, out_half, width),
        swap(other_half(core, out_half, width)),
        1,
    )

    low_ext = jnp.concatenate([jnp.where(lower, swap(past), past), low], axis=0)
    grad_all = both(own_grad)
    up_half = own_half(core, grad_all, out_cols, axis=1)

    spans = jnp.swapaxes(utt_span[:, 0], 0, 1)
    spans = both(spans).T - (y * 2 + lax.axis_index("xh")) * (CORES * count) + halo
    blocked = spans.reshape(2, -1, STRETCH)
    blocked = blocked - (jnp.arange(blocked.shape[1], dtype=jnp.int32) * STRETCH)[None, :, None]
    blocked = jnp.concatenate([blocked, blocked], axis=-1)
    middle = blocked.shape[1] // 2

    d_context = nt(grad_all, full_out).astype(BF)
    projected = nn(low_ext, full_qkv).astype(BF)
    ctx_a, dq_a, dk_a, dv_a = attention(
        0, blocked[0, :middle], blocked[1, :middle], projected, d_context[:count]
    )
    d_history = jnp.concatenate([dk_a[:halo], dv_a[:halo]], axis=1).astype(BF)
    returned = lax.ppermute(d_history, ALL, BACK)
    ctx_b, dq_b, dk_b, dv_b = attention(
        count, blocked[0, middle:], blocked[1, middle:], projected, d_context[count:]
    )
    context = jnp.concatenate([ctx_a, ctx_b], axis=0)
    all_context = in_order(lower, context, swap(context), 1)

    d_low = jnp.concatenate([dk_a[halo:] + dk_b[:halo], dv_a[halo:] + dv_b[:halo]], axis=1)
    d_low = jnp.concatenate([dq_a, d_low.astype(BF)], axis=1)
    d_last = jnp.concatenate([dk_b[halo:], dv_b[halo:]], axis=1)
    late = late_part(low_ext, dq_a, dq_b, dk_a, dk_b, dv_a, dv_b)
    late, returned, dv_a, dv_b, context = lax.optimization_barrier(
        (late, returned, dv_a, dv_b, context)
    )
    arrived = scatter(late.reshape(chips // ROWS_Y, -1, late.shape[-1]))
    first = first_part(y, all_context, up_half, low_ext, dv_a, dv_b)
    summed = first[0].astype(F32)
    for k in range(1, ROWS_Y):
        summed = summed + lax.ppermute(first[k], ALL, from_y(-k)).astype(F32)
    summed = summed.astype(BF).reshape(chips // ROWS_Y, 24, -1)
    summed, arrived, dq_b, d_low, d_last, returned = lax.optimization_barrier(
        (summed, arrived, dq_b, d_low, d_last, returned)
    )
    planes = jnp.sum(arrived.astype(F32), axis=0).reshape(ROWS_Y, -1, late.shape[-1])
    total_late = lax.dynamic_index_in_dim(planes, y, axis=0, keepdims=False)
    for k in range(1, ROWS_Y):
        away = lax.dynamic_index_in_dim(planes, (y + k) % ROWS_Y, axis=0, keepdims=False)
        total_late = total_late + lax.ppermute(away, ALL, from_y(-k))
    total_first = jnp.sum(scatter(summed).astype(F32), axis=0)
    d_proj = jnp.concatenate(
        [d_low, jnp.concatenate([dq_b, (d_last + returned.astype(F32)).astype(BF)], axis=1)], axis=0
    )

    o_rows = inner // chips // CORES
    folds = total_first[:, width - LEAD :].reshape(2, CORES * o_rows, width)
    o_total = jnp.concatenate([folds[0], folds[1]], axis=1)
    o_out = in_order(
        lower, own_half(core, o_total, o_rows), swap(other_half(core, o_total, o_rows)), 1
    )

    rows = wide // chips // CORES
    total = jnp.concatenate([total_late, total_first[:, : width - LEAD]], axis=1)
    q_kept = own_half(core, total, rows).reshape(rows, 3, width)
    q_other = swap(other_half(core, total, rows)).reshape(rows, 3, width)
    q_out = in_order(lower, q_kept, q_other, 2).reshape(rows, 3 * inner)

    partial = nn(context, full_out)
    branch = (
        own_half(core, partial, count)
        + swap(other_half(core, partial, count).astype(BF)).astype(F32)
    ).astype(BF)

    d_partial = nt(d_proj, full_qkv)
    d_normed = own_half(core, d_partial, count) + swap(
        other_half(core, d_partial, count).astype(BF)
    ).astype(F32)
    grad_in = inv_sigma * (
        d_normed
        - jnp.mean(d_normed, axis=-1, keepdims=True)
        - normed * jnp.mean(d_normed * normed, axis=-1, keepdims=True)
    )
    return (branch[None], grad_in.astype(BF)[None], q_out, o_out)


def solution(mesh):
    fine = Mesh(mesh.devices.reshape(tuple(SIZES.values())), ALL)
    dp, seq = ("z", "xl"), ("y", "xh", "c")
    rows = P(dp, seq, None)
    in_specs = (rows, rows, P(None, dp, seq), P(dp, None), P(dp, None))
    out_specs = (rows, rows, P(ALL, None), P(ALL, None))
    return jax.shard_map(body, mesh=fine, in_specs=in_specs, out_specs=out_specs, check_vma=False)
```

```python
import functools

import jax
import jax.numpy as jnp
from jax import lax
from jax.experimental import pallas as pl
from jax.experimental.pallas import tpu as pltpu
from jax.sharding import Mesh
from jax.sharding import PartitionSpec as P

HEAD_DIM = 64
STRETCH = 64
PRIOR = 4
WINDOW = (PRIOR + 1) * STRETCH
PAIR = 2 * HEAD_DIM
LEAD = 128
EPS = 1e-05

BF = jnp.bfloat16
F32 = jnp.float32


def nt(a, b):
    return lax.dot_general(a, b, (((1,), (1,)), ((), ())), preferred_element_type=F32)


def tn(a, b):
    return lax.dot_general(a, b, (((0,), (0,)), ((), ())), preferred_element_type=F32)


def nn(a, b):
    return lax.dot_general(a, b, (((1,), (0,)), ((), ())), preferred_element_type=F32)


def attend(first, lo_ref, hi_ref, proj_ref, dctx_ref, ctx_ref, dq_ref, dk_ref, dv_ref):
    width = ctx_ref.shape[1]
    blocks = ctx_ref.shape[0] // STRETCH
    dk_ref[...] = jnp.zeros_like(dk_ref)
    dv_ref[...] = jnp.zeros_like(dv_ref)
    lanes = lax.broadcasted_iota(jnp.int32, (STRETCH, PAIR), 1) < HEAD_DIM
    key_at = lax.broadcasted_iota(jnp.int32, (WINDOW, PAIR), 0)

    def stack(value):
        none = jnp.zeros_like(value)
        return jnp.concatenate(
            [jnp.where(lanes, value, none), jnp.where(lanes, none, value)], axis=0
        )

    def unstack(value):
        return jnp.where(lanes, value[:STRETCH], value[STRETCH:])

    for b in range(blocks):
        rows = pl.ds(b * STRETCH, STRETCH)
        seen = (key_at >= lo_ref[b : b + 1, :]) & (key_at < hi_ref[b : b + 1, :])
        for pair in range(width // PAIR):
            cols = pl.ds(pair * PAIR, PAIR)
            window = pl.ds(b * STRETCH, WINDOW)
            queries = stack(
                proj_ref[pl.ds(first + PRIOR * STRETCH + b * STRETCH, STRETCH), cols]
            )
            source = pl.ds(first + b * STRETCH, WINDOW)
            keys = proj_ref[source, pl.ds(width + pair * PAIR, PAIR)]
            values = proj_ref[source, pl.ds(2 * width + pair * PAIR, PAIR)]
            d_out = stack(dctx_ref[rows, cols])
            scores = jnp.where(seen, nt(keys, queries) * HEAD_DIM ** (-0.5), -1e30)
            weights = jnp.exp(scores - jnp.max(scores, axis=0, keepdims=True))
            probs = weights * (1.0 / jnp.sum(weights, axis=0, keepdims=True))
            low = probs.astype(BF)
            d_probs = nt(values, d_out)
            centre = jnp.sum(probs * d_probs, axis=0, keepdims=True)
            d_scores = (probs * (d_probs - centre) * HEAD_DIM ** (-0.5)).astype(BF)
            ctx_ref[rows, cols] = unstack(tn(low, values)).astype(BF)
            dq_ref[rows, cols] = unstack(tn(d_scores, keys)).astype(BF)
            dk_ref[window, cols] += nn(d_scores, queries)
            dv_ref[window, cols] += nn(low, d_out)


def attention(first, lo, hi, proj, d_context):
    queries, width = d_context.shape
    ext = queries + PRIOR * STRETCH
    whole = pl.BlockSpec(memory_space=pltpu.VMEM)
    return pl.pallas_call(
        functools.partial(attend, first),
        in_specs=[whole] * 4,
        out_specs=[whole] * 4,
        out_shape=[
            jax.ShapeDtypeStruct((queries, width), BF),
            jax.ShapeDtypeStruct((queries, width), BF),
            jax.ShapeDtypeStruct((ext, width), F32),
            jax.ShapeDtypeStruct((ext, width), F32),
        ],
        compiler_params=pltpu.CompilerParams(vmem_limit_bytes=40 * 1024 * 1024),
        name="attend",
    )(lo, hi, proj, d_context)


def normalize(inputs):
    widened = inputs.astype(F32)
    centered = widened - jnp.mean(widened, axis=-1, keepdims=True)
    inv_sigma = lax.rsqrt(jnp.mean(centered * centered, axis=-1, keepdims=True) + EPS)
    return (centered * inv_sigma, inv_sigma)


SIZES = {"z": 4, "xl": 2, "y": 4, "xh": 2, "c": 2}
ALL = tuple(SIZES)
DP, CHIPS, CORES, ROWS_Y = 8, 8, 2, 4


def device(dp, t, c):
    return (dp * CHIPS + t) * CORES + c


EVERY = [(d, t, c) for d in range(DP) for t in range(CHIPS) for c in range(CORES)]
SWAP = [(device(d, t, c), device(d, t, 1 - c)) for d, t, c in EVERY]
ONWARD = [(device(d, t, 1), device(d, t + 1, 1)) for d, t, c in EVERY if c and t + 1 < CHIPS]
BACK = [(device(d, t, c), device(d, t - 1, c)) for d, t, c in EVERY if t > 0]


def from_y(by):
    return [(device(d, (t + 2 * by) % CHIPS, c), device(d, t, c)) for d, t, c in EVERY]


def swap(value):
    return lax.ppermute(value, ALL, SWAP)


def fill(d_ref, at, early, late, halo, take):
    count = d_ref.shape[0] - early.shape[0]
    cols = slice(at, at + take.stop - take.start)
    d_ref[:halo, cols] = early[:halo, take].astype(BF)
    d_ref[halo : halo + count, cols] = (early[halo:, take] + late[:halo, take]).astype(BF)
    d_ref[halo + count :, cols] = late[halo:, take].astype(BF)


def late_gradients(low_ref, dq_a, dq_b, dk_a, dk_b, dv_a, dv_b, late_ref, d_ref):
    @pl.when(pl.program_id(0) == 0)
    def _():
        count, width = dq_a.shape
        halo = d_ref.shape[0] - 2 * count
        d_ref[:halo, :width] = jnp.zeros((halo, width), BF)
        d_ref[halo : halo + count, :width] = dq_a[...]
        d_ref[halo + count :, :width] = dq_b[...]
        fill(d_ref, width, dk_a, dk_b, halo, slice(0, width))
        fill(d_ref, 2 * width, dv_a, dv_b, halo, slice(0, LEAD))

    grad = tn(low_ref[...], d_ref[...])
    for j in range(2 * CHIPS):
        dp, y, xh = j // CHIPS, j % CHIPS // 2, j % 2
        late_ref[dp, xh, y] = grad[j * 24 : j * 24 + 24].astype(BF)


def first_gradients(
    y_ref, ctx_ref, up_ref, low_ref, dv_a, dv_b, *rest
):
    outs, (out_scr, d_ref, grad_scr, fold_scr) = rest[:ROWS_Y], rest[ROWS_Y:]
    step = pl.program_id(0)
    width = dv_a.shape[1]

    @pl.when(step == 0)
    def _():
        out_scr[...] = tn(ctx_ref[...], up_ref[...]).astype(BF)
        halo = d_ref.shape[0] - ctx_ref.shape[0]
        fill(d_ref, 0, dv_a, dv_b, halo, slice(LEAD, width))

    own = 2 * CHIPS
    to = lax.broadcasted_iota(jnp.int32, (own * 24, own * 12), 0)
    at = lax.broadcasted_iota(jnp.int32, (own * 24, own * 12), 1)
    base, slot = to // 24 * 12, to % 24
    rows = out_scr[pl.ds(pl.multiple_of(step * own * 12, 64), own * 12), :]
    folded = jnp.zeros((own * 24, width), F32)
    for q in range(2):
        pick = (slot >= q * 12) & (slot < q * 12 + 12) & (at == base + slot - q * 12)
        folded += nn(pick.astype(BF), rows[:, q * width : (q + 1) * width])
    fold_scr[...] = folded
    grad_scr[...] = tn(low_ref[...], d_ref[...])
    for k in range(ROWS_Y):
        y = lax.rem(y_ref[0] + k, ROWS_Y)
        for dp in range(2):
            for xh in range(2):
                chunk = pl.ds(pl.multiple_of(((dp * ROWS_Y + y) * 2 + xh) * 24, 8), 24)
                outs[k][dp, xh] = jnp.concatenate(
                    [grad_scr[chunk, :], fold_scr[chunk, :]], axis=1
                ).astype(BF)


def whole(value):
    return pl.BlockSpec(value.shape, lambda i: (0, 0))


def late_part(low_ext, *parts):
    ext, wide = low_ext.shape
    columns = 2 * parts[0].shape[1] + LEAD
    steps = DP // 2
    return pl.pallas_call(
        late_gradients,
        grid=(steps,),
        in_specs=[
            pl.BlockSpec((ext, wide // steps), lambda i: (0, i)),
            *[whole(part) for part in parts],
        ],
        out_specs=pl.BlockSpec((2, 2, ROWS_Y, 24, columns), lambda i: (i, 0, 0, 0, 0)),
        out_shape=jax.ShapeDtypeStruct((DP, 2, ROWS_Y, 24, columns), BF),
        scratch_shapes=[pltpu.VMEM((ext, columns), BF)],
        compiler_params=pltpu.CompilerParams(vmem_limit_bytes=48 * 1024 * 1024),
        name="late_gradients",
    )(low_ext, *parts)


def first_part(y, context, up_half, low_ext, dv_a, dv_b):
    ext, wide = low_ext.shape
    width = dv_a.shape[1]
    steps = DP // 2
    columns = 2 * width - LEAD
    block = pl.BlockSpec((2, 2, 24, columns), lambda i: (i, 0, 0, 0))
    return pl.pallas_call(
        first_gradients,
        grid=(steps,),
        in_specs=[
            pl.BlockSpec(memory_space=pltpu.SMEM),
            whole(context),
            whole(up_half),
            pl.BlockSpec((ext, wide // steps), lambda i: (0, i)),
            whole(dv_a),
            whole(dv_b),
        ],
        out_specs=[block] * ROWS_Y,
        out_shape=[jax.ShapeDtypeStruct((DP, 2, 24, columns), BF)] * ROWS_Y,
        scratch_shapes=[
            pltpu.VMEM((context.shape[1], up_half.shape[1]), BF),
            pltpu.VMEM((ext, width - LEAD), BF),
            pltpu.VMEM((2 * CHIPS * 24, width - LEAD), F32),
            pltpu.VMEM((2 * CHIPS * 24, width), F32),
        ],
        compiler_params=pltpu.CompilerParams(vmem_limit_bytes=48 * 1024 * 1024),
        name="first_gradients",
    )(y.reshape(1), context, up_half, low_ext, dv_a, dv_b)


def own_half(core, value, size, axis=0):
    return lax.dynamic_slice_in_dim(value, core * size, size, axis=axis)


def other_half(core, value, size, axis=0):
    return lax.dynamic_slice_in_dim(value, (1 - core) * size, size, axis=axis)


def in_order(lower, own, other, axis):
    return jnp.concatenate(
        [jnp.where(lower, own, other), jnp.where(lower, other, own)], axis=axis
    )


def scatter(chunks):
    return lax.all_to_all(chunks, ("z", "xl", "xh"), 0, 0, tiled=True)


def copies(shard):
    return jnp.broadcast_to(shard[None], (DP,) + shard.shape)


def gather(shards):
    return lax.all_to_all(shards, ("z", "xl"), 0, 0, tiled=True)


def body(frames, upstream, utt_span, w_qkv, w_out):
    core = lax.axis_index("c")
    lower = core == 0
    own_frames = frames[0]
    own_grad = upstream[0]
    count, wide = own_frames.shape
    inner = w_qkv.shape[1] // 3
    width = inner // CORES
    halo = PRIOR * STRETCH
    chips = DP * CHIPS
    out_cols = wide // CORES

    def both(own):
        return in_order(lower, own, swap(own), 0)

    y = lax.axis_index("y")
    mine = jnp.concatenate(
        [own_half(core, w_qkv[:, k * inner : (k + 1) * inner], width, axis=1) for k in range(3)],
        axis=1,
    )
    out_mine = own_half(core, w_out, out_cols, axis=1)
    deep = mine.shape[0]
    direct = deep * 2 // 3
    low_rows = deep // 3
    tail = out_mine[low_rows:]
    folded = jnp.concatenate(
        [out_mine[:low_rows], jnp.concatenate([tail[:, :width], tail[:, width:]], axis=0)],
        axis=1,
    )
    indirect = jnp.concatenate(
        [
            mine[direct:].reshape(ROWS_Y, -1, 3 * width),
            folded.reshape(ROWS_Y, -1, 3 * width),
        ],
        axis=1,
    )
    pieces = copies(lax.dynamic_index_in_dim(indirect, y, axis=0, keepdims=False))
    shards = copies(mine[:direct])
    own_frames, own_grad, pieces = lax.optimization_barrier((own_frames, own_grad, pieces))
    normed, inv_sigma = normalize(own_frames)
    own_low = normed.astype(BF)
    own_low, other_low = lax.optimization_barrier((own_low, swap(own_low)))
    low = in_order(lower, own_low, other_low, 0)
    past = lax.ppermute(own_low, ALL, ONWARD)
    quarter = gather(pieces)
    shards, quarter, past = lax.optimization_barrier((shards, quarter, past))
    full_direct = gather(shards)
    quarters = jnp.zeros((ROWS_Y,) + quarter.shape, BF)
    for k in range(ROWS_Y):
        got = quarter if k == 0 else lax.ppermute(quarter, ALL, from_y(k))
        quarters = lax.dynamic_update_index_in_dim(quarters, got, (y + k) % ROWS_Y, 0)
    qkv_rows = (deep - direct) // ROWS_Y
    full_qkv = jnp.concatenate(
        [full_direct] + [quarters[i, :, :qkv_rows] for i in range(ROWS_Y)], axis=1
    ).reshape(wide, 3 * width)
    unfolded = jnp.concatenate([quarters[i, :, qkv_rows:] for i in range(ROWS_Y)], axis=1)
    rest = unfolded[:, :, out_cols:]
    half = rest.shape[1] // 2
    out_half = jnp.concatenate(
        [
            unfolded[:, :, :out_cols],
            jnp.concatenate([rest[:, :half], rest[:, half:]], axis=2),
        ],
        axis=1,
    ).reshape(inner, out_cols)
    full_out = in_order(
        lower,
        own_half(core, out_half, width),
        swap(other_half(core, out_half, width)),
        1,
    )

    low_ext = jnp.concatenate([jnp.where(lower, swap(past), past), low], axis=0)
    grad_all = both(own_grad)
    up_half = own_half(core, grad_all, out_cols, axis=1)

    spans = jnp.swapaxes(utt_span[:, 0], 0, 1)
    spans = both(spans).T - (y * 2 + lax.axis_index("xh")) * (CORES * count) + halo
    blocked = spans.reshape(2, -1, STRETCH)
    blocked = blocked - (jnp.arange(blocked.shape[1], dtype=jnp.int32) * STRETCH)[None, :, None]
    blocked = jnp.concatenate([blocked, blocked], axis=-1)
    middle = blocked.shape[1] // 2

    d_context = nt(grad_all, full_out).astype(BF)
    projected = nn(low_ext, full_qkv).astype(BF)
    ctx_a, dq_a, dk_a, dv_a = attention(
        0, blocked[0, :middle], blocked[1, :middle], projected, d_context[:count]
    )
    d_history = jnp.concatenate([dk_a[:halo], dv_a[:halo]], axis=1).astype(BF)
    returned = lax.ppermute(d_history, ALL, BACK)
    ctx_b, dq_b, dk_b, dv_b = attention(
        count, blocked[0, middle:], blocked[1, middle:], projected, d_context[count:]
    )
    context = jnp.concatenate([ctx_a, ctx_b], axis=0)
    all_context = in_order(lower, context, swap(context), 1)

    d_low = jnp.concatenate([dk_a[halo:] + dk_b[:halo], dv_a[halo:] + dv_b[:halo]], axis=1)
    d_low = jnp.concatenate([dq_a, d_low.astype(BF)], axis=1)
    d_last = jnp.concatenate([dk_b[halo:], dv_b[halo:]], axis=1)
    late = late_part(low_ext, dq_a, dq_b, dk_a, dk_b, dv_a, dv_b)
    late, returned, dv_a, dv_b, context = lax.optimization_barrier(
        (late, returned, dv_a, dv_b, context)
    )
    arrived = scatter(late.reshape(chips // ROWS_Y, -1, late.shape[-1]))
    first = first_part(y, all_context, up_half, low_ext, dv_a, dv_b)
    summed = first[0].astype(F32)
    for k in range(1, ROWS_Y):
        summed = summed + lax.ppermute(first[k], ALL, from_y(-k)).astype(F32)
    summed = summed.astype(BF).reshape(chips // ROWS_Y, 24, -1)
    summed, arrived, dq_b, d_low, d_last, returned = lax.optimization_barrier(
        (summed, arrived, dq_b, d_low, d_last, returned)
    )
    planes = jnp.sum(arrived.astype(F32), axis=0).reshape(ROWS_Y, -1, late.shape[-1])
    total_late = lax.dynamic_index_in_dim(planes, y, axis=0, keepdims=False)
    for k in range(1, ROWS_Y):
        away = lax.dynamic_index_in_dim(planes, (y + k) % ROWS_Y, axis=0, keepdims=False)
        total_late = total_late + lax.ppermute(away, ALL, from_y(-k))
    total_first = jnp.sum(scatter(summed).astype(F32), axis=0)
    d_proj = jnp.concatenate(
        [d_low, jnp.concatenate([dq_b, (d_last + returned.astype(F32)).astype(BF)], axis=1)], axis=0
    )

    o_rows = inner // chips // CORES
    folds = total_first[:, width - LEAD :].reshape(2, CORES * o_rows, width)
    o_total = jnp.concatenate([folds[0], folds[1]], axis=1)
    o_out = in_order(
        lower, own_half(core, o_total, o_rows), swap(other_half(core, o_total, o_rows)), 1
    )

    rows = wide // chips // CORES
    total = jnp.concatenate([total_late, total_first[:, : width - LEAD]], axis=1)
    q_kept = own_half(core, total, rows).reshape(rows, 3, width)
    q_other = swap(other_half(core, total, rows)).reshape(rows, 3, width)
    q_out = in_order(lower, q_kept, q_other, 2).reshape(rows, 3 * inner)

    partial = nn(context, full_out)
    branch = (
        own_half(core, partial, count)
        + swap(other_half(core, partial, count).astype(BF)).astype(F32)
    ).astype(BF)

    d_partial = nt(d_proj, full_qkv)
    d_normed = own_half(core, d_partial, count) + swap(
        other_half(core, d_partial, count).astype(BF)
    ).astype(F32)
    grad_in = inv_sigma * (
        d_normed
        - jnp.mean(d_normed, axis=-1, keepdims=True)
        - normed * jnp.mean(d_normed * normed, axis=-1, keepdims=True)
    )
    return (branch[None], grad_in.astype(BF)[None], q_out, o_out)


def solution(mesh):
    fine = Mesh(mesh.devices.reshape(tuple(SIZES.values())), ALL)
    dp, seq = ("z", "xl"), ("y", "xh", "c")
    rows = P(dp, seq, None)
    in_specs = (rows, rows, P(None, dp, seq), P(dp, None), P(dp, None))
    out_specs = (rows, rows, P(ALL, None), P(ALL, None))
    return jax.shard_map(body, mesh=fine, in_specs=in_specs, out_specs=out_specs, check_vma=False)
```

```python
import functools

import jax
import jax.numpy as jnp
from jax import lax
from jax.experimental import pallas as pl
from jax.experimental.pallas import tpu as pltpu
from jax.sharding import Mesh
from jax.sharding import PartitionSpec as P

HEAD_DIM = 64
STRETCH = 64
PRIOR = 4
WINDOW = (PRIOR + 1) * STRETCH
PAIR = 2 * HEAD_DIM
LEAD = 128
EPS = 1e-05

BF = jnp.bfloat16
F32 = jnp.float32


def nt(a, b):
    return lax.dot_general(a, b, (((1,), (1,)), ((), ())), preferred_element_type=F32)


def tn(a, b):
    return lax.dot_general(a, b, (((0,), (0,)), ((), ())), preferred_element_type=F32)


def nn(a, b):
    return lax.dot_general(a, b, (((1,), (0,)), ((), ())), preferred_element_type=F32)


def attend(first, lo_ref, hi_ref, proj_ref, dctx_ref, ctx_ref, dq_ref, dk_ref, dv_ref):
    width = ctx_ref.shape[1]
    blocks = ctx_ref.shape[0] // STRETCH
    dk_ref[...] = jnp.zeros_like(dk_ref)
    dv_ref[...] = jnp.zeros_like(dv_ref)
    lanes = lax.broadcasted_iota(jnp.int32, (STRETCH, PAIR), 1) < HEAD_DIM
    key_at = lax.broadcasted_iota(jnp.int32, (WINDOW, PAIR), 0)

    def stack(value):
        none = jnp.zeros_like(value)
        return jnp.concatenate(
            [jnp.where(lanes, value, none), jnp.where(lanes, none, value)], axis=0
        )

    def unstack(value):
        return jnp.where(lanes, value[:STRETCH], value[STRETCH:])

    for b in range(blocks):
        rows = pl.ds(b * STRETCH, STRETCH)
        seen = (key_at >= lo_ref[b : b + 1, :]) & (key_at < hi_ref[b : b + 1, :])
        for pair in range(width // PAIR):
            cols = pl.ds(pair * PAIR, PAIR)
            window = pl.ds(b * STRETCH, WINDOW)
            queries = stack(
                proj_ref[pl.ds(first + PRIOR * STRETCH + b * STRETCH, STRETCH), cols]
            )
            source = pl.ds(first + b * STRETCH, WINDOW)
            keys = proj_ref[source, pl.ds(width + pair * PAIR, PAIR)]
            values = proj_ref[source, pl.ds(2 * width + pair * PAIR, PAIR)]
            d_out = stack(dctx_ref[rows, cols])
            scores = jnp.where(seen, nt(keys, queries) * HEAD_DIM ** (-0.5), -1e30)
            weights = jnp.exp(scores - jnp.max(scores, axis=0, keepdims=True))
            probs = weights * (1.0 / jnp.sum(weights, axis=0, keepdims=True))
            low = probs.astype(BF)
            d_probs = nt(values, d_out)
            centre = jnp.sum(probs * d_probs, axis=0, keepdims=True)
            d_scores = (probs * (d_probs - centre) * HEAD_DIM ** (-0.5)).astype(BF)
            ctx_ref[rows, cols] = unstack(tn(low, values)).astype(BF)
            dq_ref[rows, cols] = unstack(tn(d_scores, keys)).astype(BF)
            dk_ref[window, cols] += nn(d_scores, queries)
            dv_ref[window, cols] += nn(low, d_out)


def attention(first, lo, hi, proj, d_context):
    queries, width = d_context.shape
    ext = queries + PRIOR * STRETCH
    whole = pl.BlockSpec(memory_space=pltpu.VMEM)
    return pl.pallas_call(
        functools.partial(attend, first),
        in_specs=[whole] * 4,
        out_specs=[whole] * 4,
        out_shape=[
            jax.ShapeDtypeStruct((queries, width), BF),
            jax.ShapeDtypeStruct((queries, width), BF),
            jax.ShapeDtypeStruct((ext, width), F32),
            jax.ShapeDtypeStruct((ext, width), F32),
        ],
        compiler_params=pltpu.CompilerParams(vmem_limit_bytes=40 * 1024 * 1024),
        name="attend",
    )(lo, hi, proj, d_context)


def normalize(inputs):
    widened = inputs.astype(F32)
    centered = widened - jnp.mean(widened, axis=-1, keepdims=True)
    inv_sigma = lax.rsqrt(jnp.mean(centered * centered, axis=-1, keepdims=True) + EPS)
    return (centered * inv_sigma, inv_sigma)


SIZES = {"z": 4, "xl": 2, "y": 4, "xh": 2, "c": 2}
ALL = tuple(SIZES)
DP, CHIPS, CORES, ROWS_Y = 8, 8, 2, 4


def device(dp, t, c):
    return (dp * CHIPS + t) * CORES + c


EVERY = [(d, t, c) for d in range(DP) for t in range(CHIPS) for c in range(CORES)]
SWAP = [(device(d, t, c), device(d, t, 1 - c)) for d, t, c in EVERY]
ONWARD = [(device(d, t, 1), device(d, t + 1, 1)) for d, t, c in EVERY if c and t + 1 < CHIPS]
BACK = [(device(d, t, c), device(d, t - 1, c)) for d, t, c in EVERY if t > 0]


def from_y(by):
    return [(device(d, (t + 2 * by) % CHIPS, c), device(d, t, c)) for d, t, c in EVERY]


def swap(value):
    return lax.ppermute(value, ALL, SWAP)


def fill(d_ref, at, early, late, halo, take):
    count = d_ref.shape[0] - early.shape[0]
    cols = slice(at, at + take.stop - take.start)
    d_ref[:halo, cols] = early[:halo, take].astype(BF)
    d_ref[halo : halo + count, cols] = (early[halo:, take] + late[:halo, take]).astype(BF)
    d_ref[halo + count :, cols] = late[halo:, take].astype(BF)


def late_gradients(low_ref, dq_a, dq_b, dk_a, dk_b, dv_a, dv_b, late_ref, d_ref):
    @pl.when(pl.program_id(0) == 0)
    def _():
        count, width = dq_a.shape
        halo = d_ref.shape[0] - 2 * count
        d_ref[:halo, :width] = jnp.zeros((halo, width), BF)
        d_ref[halo : halo + count, :width] = dq_a[...]
        d_ref[halo + count :, :width] = dq_b[...]
        fill(d_ref, width, dk_a, dk_b, halo, slice(0, width))
        fill(d_ref, 2 * width, dv_a, dv_b, halo, slice(0, LEAD))

    grad = tn(low_ref[...], d_ref[...])
    for j in range(2 * CHIPS):
        dp, y, xh = j // CHIPS, j % CHIPS // 2, j % 2
        late_ref[dp, xh, y] = grad[j * 24 : j * 24 + 24].astype(BF)


def first_gradients(
    y_ref, ctx_ref, up_ref, low_ref, dv_a, dv_b, *rest
):
    outs, (out_scr, d_ref, grad_scr, fold_scr) = rest[:ROWS_Y], rest[ROWS_Y:]
    step = pl.program_id(0)
    width = dv_a.shape[1]

    @pl.when(step == 0)
    def _():
        out_scr[...] = tn(ctx_ref[...], up_ref[...]).astype(BF)
        halo = d_ref.shape[0] - ctx_ref.shape[0]
        fill(d_ref, 0, dv_a, dv_b, halo, slice(LEAD, width))

    own = 2 * CHIPS
    to = lax.broadcasted_iota(jnp.int32, (own * 24, own * 12), 0)
    at = lax.broadcasted_iota(jnp.int32, (own * 24, own * 12), 1)
    base, slot = to // 24 * 12, to % 24
    rows = out_scr[pl.ds(pl.multiple_of(step * own * 12, 64), own * 12), :]
    folded = jnp.zeros((own * 24, width), F32)
    for q in range(2):
        pick = (slot >= q * 12) & (slot < q * 12 + 12) & (at == base + slot - q * 12)
        folded += nn(pick.astype(BF), rows[:, q * width : (q + 1) * width])
    fold_scr[...] = folded
    grad_scr[...] = tn(low_ref[...], d_ref[...])
    for k in range(ROWS_Y):
        y = lax.rem(y_ref[0] + k, ROWS_Y)
        for dp in range(2):
            for xh in range(2):
                chunk = pl.ds(pl.multiple_of(((dp * ROWS_Y + y) * 2 + xh) * 24, 8), 24)
                outs[k][dp, xh] = jnp.concatenate(
                    [grad_scr[chunk, :], fold_scr[chunk, :]], axis=1
                ).astype(BF)


def whole(value):
    return pl.BlockSpec(value.shape, lambda i: (0, 0))


def late_part(low_ext, *parts):
    ext, wide = low_ext.shape
    columns = 2 * parts[0].shape[1] + LEAD
    steps = DP // 2
    return pl.pallas_call(
        late_gradients,
        grid=(steps,),
        in_specs=[
            pl.BlockSpec((ext, wide // steps), lambda i: (0, i)),
            *[whole(part) for part in parts],
        ],
        out_specs=pl.BlockSpec((2, 2, ROWS_Y, 24, columns), lambda i: (i, 0, 0, 0, 0)),
        out_shape=jax.ShapeDtypeStruct((DP, 2, ROWS_Y, 24, columns), BF),
        scratch_shapes=[pltpu.VMEM((ext, columns), BF)],
        compiler_params=pltpu.CompilerParams(vmem_limit_bytes=48 * 1024 * 1024),
        name="late_gradients",
    )(low_ext, *parts)


def first_part(y, context, up_half, low_ext, dv_a, dv_b):
    ext, wide = low_ext.shape
    width = dv_a.shape[1]
    steps = DP // 2
    columns = 2 * width - LEAD
    block = pl.BlockSpec((2, 2, 24, columns), lambda i: (i, 0, 0, 0))
    return pl.pallas_call(
        first_gradients,
        grid=(steps,),
        in_specs=[
            pl.BlockSpec(memory_space=pltpu.SMEM),
            whole(context),
            whole(up_half),
            pl.BlockSpec((ext, wide // steps), lambda i: (0, i)),
            whole(dv_a),
            whole(dv_b),
        ],
        out_specs=[block] * ROWS_Y,
        out_shape=[jax.ShapeDtypeStruct((DP, 2, 24, columns), BF)] * ROWS_Y,
        scratch_shapes=[
            pltpu.VMEM((context.shape[1], up_half.shape[1]), BF),
            pltpu.VMEM((ext, width - LEAD), BF),
            pltpu.VMEM((2 * CHIPS * 24, width - LEAD), F32),
            pltpu.VMEM((2 * CHIPS * 24, width), F32),
        ],
        compiler_params=pltpu.CompilerParams(vmem_limit_bytes=48 * 1024 * 1024),
        name="first_gradients",
    )(y.reshape(1), context, up_half, low_ext, dv_a, dv_b)


def own_half(core, value, size, axis=0):
    return lax.dynamic_slice_in_dim(value, core * size, size, axis=axis)


def other_half(core, value, size, axis=0):
    return lax.dynamic_slice_in_dim(value, (1 - core) * size, size, axis=axis)


def in_order(lower, own, other, axis):
    return jnp.concatenate(
        [jnp.where(lower, own, other), jnp.where(lower, other, own)], axis=axis
    )


def scatter(chunks):
    return lax.all_to_all(chunks, ("z", "xl", "xh"), 0, 0, tiled=True)


def copies(shard):
    return jnp.broadcast_to(shard[None], (DP,) + shard.shape)


def gather(shards):
    return lax.all_to_all(shards, ("z", "xl"), 0, 0, tiled=True)


def body(frames, upstream, utt_span, w_qkv, w_out):
    core = lax.axis_index("c")
    lower = core == 0
    own_frames = frames[0]
    own_grad = upstream[0]
    count, wide = own_frames.shape
    inner = w_qkv.shape[1] // 3
    width = inner // CORES
    halo = PRIOR * STRETCH
    chips = DP * CHIPS
    out_cols = wide // CORES

    def both(own):
        return in_order(lower, own, swap(own), 0)

    y = lax.axis_index("y")
    mine = jnp.concatenate(
        [own_half(core, w_qkv[:, k * inner : (k + 1) * inner], width, axis=1) for k in range(3)],
        axis=1,
    )
    out_mine = own_half(core, w_out, out_cols, axis=1)
    deep = mine.shape[0]
    direct = deep * 2 // 3
    low_rows = deep // 3
    tail = out_mine[low_rows:]
    folded = jnp.concatenate(
        [out_mine[:low_rows], jnp.concatenate([tail[:, :width], tail[:, width:]], axis=0)],
        axis=1,
    )
    indirect = jnp.concatenate(
        [
            mine[direct:].reshape(ROWS_Y, -1, 3 * width),
            folded.reshape(ROWS_Y, -1, 3 * width),
        ],
        axis=1,
    )
    pieces = copies(lax.dynamic_index_in_dim(indirect, y, axis=0, keepdims=False))
    shards = copies(mine[:direct])
    own_frames, own_grad, pieces = lax.optimization_barrier((own_frames, own_grad, pieces))
    normed, inv_sigma = normalize(own_frames)
    own_low = normed.astype(BF)
    own_low, other_low = lax.optimization_barrier((own_low, swap(own_low)))
    low = in_order(lower, own_low, other_low, 0)
    past = lax.ppermute(own_low, ALL, ONWARD)
    quarter = gather(pieces)
    shards, quarter, past = lax.optimization_barrier((shards, quarter, past))
    full_direct = gather(shards)
    quarters = jnp.zeros((ROWS_Y,) + quarter.shape, BF)
    for k in range(ROWS_Y):
        got = quarter if k == 0 else lax.ppermute(quarter, ALL, from_y(k))
        quarters = lax.dynamic_update_index_in_dim(quarters, got, (y + k) % ROWS_Y, 0)
    qkv_rows = (deep - direct) // ROWS_Y
    full_qkv = jnp.concatenate(
        [full_direct] + [quarters[i, :, :qkv_rows] for i in range(ROWS_Y)], axis=1
    ).reshape(wide, 3 * width)
    unfolded = jnp.concatenate([quarters[i, :, qkv_rows:] for i in range(ROWS_Y)], axis=1)
    rest = unfolded[:, :, out_cols:]
    half = rest.shape[1] // 2
    out_half = jnp.concatenate(
        [
            unfolded[:, :, :out_cols],
            jnp.concatenate([rest[:, :half], rest[:, half:]], axis=2),
        ],
        axis=1,
    ).reshape(inner, out_cols)
    full_out = in_order(
        lower,
        own_half(core, out_half, width),
        swap(other_half(core, out_half, width)),
        1,
    )

    low_ext = jnp.concatenate([jnp.where(lower, swap(past), past), low], axis=0)
    grad_all = both(own_grad)
    up_half = own_half(core, grad_all, out_cols, axis=1)

    spans = jnp.swapaxes(utt_span[:, 0], 0, 1)
    spans = both(spans).T - (y * 2 + lax.axis_index("xh")) * (CORES * count) + halo
    blocked = spans.reshape(2, -1, STRETCH)
    blocked = blocked - (jnp.arange(blocked.shape[1], dtype=jnp.int32) * STRETCH)[None, :, None]
    blocked = jnp.concatenate([blocked, blocked], axis=-1)
    middle = blocked.shape[1] // 2

    d_context = nt(grad_all, full_out).astype(BF)
    projected = nn(low_ext, full_qkv).astype(BF)
    ctx_a, dq_a, dk_a, dv_a = attention(
        0, blocked[0, :middle], blocked[1, :middle], projected, d_context[:count]
    )
    d_history = jnp.concatenate([dk_a[:halo], dv_a[:halo]], axis=1).astype(BF)
    returned = lax.ppermute(d_history, ALL, BACK)
    ctx_b, dq_b, dk_b, dv_b = attention(
        count, blocked[0, middle:], blocked[1, middle:], projected, d_context[count:]
    )
    context = jnp.concatenate([ctx_a, ctx_b], axis=0)
    all_context = in_order(lower, context, swap(context), 1)

    d_low = jnp.concatenate([dk_a[halo:] + dk_b[:halo], dv_a[halo:] + dv_b[:halo]], axis=1)
    d_low = jnp.concatenate([dq_a, d_low.astype(BF)], axis=1)
    d_last = jnp.concatenate([dk_b[halo:], dv_b[halo:]], axis=1)
    late = late_part(low_ext, dq_a, dq_b, dk_a, dk_b, dv_a, dv_b)
    late, returned, dv_a, dv_b, context = lax.optimization_barrier(
        (late, returned, dv_a, dv_b, context)
    )
    arrived = scatter(late.reshape(chips // ROWS_Y, -1, late.shape[-1]))
    first = first_part(y, all_context, up_half, low_ext, dv_a, dv_b)
    summed = first[0].astype(F32)
    for k in range(1, ROWS_Y):
        summed = summed + lax.ppermute(first[k], ALL, from_y(-k)).astype(F32)
    summed = summed.astype(BF).reshape(chips // ROWS_Y, 24, -1)
    summed, arrived, dq_b, d_low, d_last, returned = lax.optimization_barrier(
        (summed, arrived, dq_b, d_low, d_last, returned)
    )
    planes = jnp.sum(arrived.astype(F32), axis=0).reshape(ROWS_Y, -1, late.shape[-1])
    total_late = lax.dynamic_index_in_dim(planes, y, axis=0, keepdims=False)
    for k in range(1, ROWS_Y):
        away = lax.dynamic_index_in_dim(planes, (y + k) % ROWS_Y, axis=0, keepdims=False)
        total_late = total_late + lax.ppermute(away, ALL, from_y(-k))
    total_first = jnp.sum(scatter(summed).astype(F32), axis=0)
    d_proj = jnp.concatenate(
        [d_low, jnp.concatenate([dq_b, (d_last + returned.astype(F32)).astype(BF)], axis=1)], axis=0
    )

    o_rows = inner // chips // CORES
    folds = total_first[:, width - LEAD :].reshape(2, CORES * o_rows, width)
    o_total = jnp.concatenate([folds[0], folds[1]], axis=1)
    o_out = in_order(
        lower, own_half(core, o_total, o_rows), swap(other_half(core, o_total, o_rows)), 1
    )

    rows = wide // chips // CORES
    total = jnp.concatenate([total_late, total_first[:, : width - LEAD]], axis=1)
    q_kept = own_half(core, total, rows)
    q_other = swap(other_half(core, total, rows))
    lower_q, upper_q = jnp.where(lower, q_kept, q_other), jnp.where(lower, q_other, q_kept)
    pieces = []
    for k in range(3):
        pieces += [part[:, k * width : (k + 1) * width] for part in (lower_q, upper_q)]
    q_out = jnp.concatenate(pieces, axis=1)

    partial = nn(context, full_out)
    branch = (
        own_half(core, partial, count)
        + swap(other_half(core, partial, count).astype(BF)).astype(F32)
    ).astype(BF)

    d_partial = nt(d_proj, full_qkv)
    d_normed = own_half(core, d_partial, count) + swap(
        other_half(core, d_partial, count).astype(BF)
    ).astype(F32)
    grad_in = inv_sigma * (
        d_normed
        - jnp.mean(d_normed, axis=-1, keepdims=True)
        - normed * jnp.mean(d_normed * normed, axis=-1, keepdims=True)
    )
    return (branch[None], grad_in.astype(BF)[None], q_out, o_out)


def solution(mesh):
    fine = Mesh(mesh.devices.reshape(tuple(SIZES.values())), ALL)
    dp, seq = ("z", "xl"), ("y", "xh", "c")
    rows = P(dp, seq, None)
    in_specs = (rows, rows, P(None, dp, seq), P(dp, None), P(dp, None))
    out_specs = (rows, rows, P(ALL, None), P(ALL, None))
    return jax.shard_map(body, mesh=fine, in_specs=in_specs, out_specs=out_specs, check_vma=False)
```
